512 devices in a mesh: seq: 32 (over z, core), head: 16 (over y, x).
Axes of the slice: x: 4, y: 4, z: 16, core: 2. Of those that a mesh axis runs over, the one named last changes fastest.
Arguments:
- inputs: float32 [131072, 2048], P('seq', 'head'), may hold values from -0.8 to 0.8
- b_proj: float32 [131072, 256], P('seq', 'head'), may hold values from -0.5 to 0.5
- c_proj: float32 [131072, 256], P('seq', 'head'), may hold values from -0.5 to 0.5
- log_decay: float32 [131072, 32], P('seq', 'head'), may hold values from -2 to 0, as said below
Outputs:
- outputs: float32 [131072, 2048], P('seq', 'head')
The draws below stay inside these ranges and needn't reach their ends.
Inputs may be any that keep to these rules, and one draw needn't show every extreme that they name: log_decay is negative.
All inputs are finite; a program needn't handle non-finite values.
Results may differ from the reference program's by a relative error of at most 0.00011.
Values sent between devices are 32-bit elements; how exact they have to be, the bound alone decides.
A program may use at most 128 MiB of HBM per device.

```python
import jax
import jax.numpy as jnp
from jax import lax

P_SIZE = 64
NSTATE = 256
BLOCK_LEN = 256
HEADS = 32
HALF = 2048
TOKENS = 131072
N_SEQ = 32


def draw_log_decay(key, part):
    key = jax.random.fold_in(key, 11)
    keys = jax.random.split(key, 7)
    fast_share = 0.5
    chooser = jax.random.uniform(keys[0], (HEADS,))
    slow_rate = jnp.exp(jax.random.uniform(keys[1], (HEADS,), minval=jnp.log(0.02 / TOKENS), maxval=jnp.log(0.3 / TOKENS)))
    fast_rate = jnp.exp(jax.random.uniform(keys[2], (HEADS,), minval=jnp.log(1.0 / 60.0), maxval=jnp.log(1.0 / 25.0)))
    rates = jnp.where(chooser < fast_share, fast_rate, slow_rate)
    block_count = TOKENS // HALF
    block_factor = jnp.exp(jax.random.uniform(keys[3], (block_count, 1, HEADS), minval=jnp.log(0.5), maxval=jnp.log(2.0)))
    token_factor = jnp.exp(jax.random.uniform(keys[4], (block_count, HALF, HEADS), minval=jnp.log(0.5), maxval=jnp.log(2.0)))
    gentle_waveform = (rates[None, None, :] * block_factor * token_factor).reshape(TOKENS, HEADS)
    impulse_indices = jax.random.randint(keys[5], (3,), 0, TOKENS)
    impulse_amplitudes = jax.random.uniform(keys[6], (3,), minval=0.22, maxval=0.45)
    impulse_locations = jnp.arange(TOKENS)[:, None]
    impulse_train = jnp.sum(jnp.where(impulse_locations == impulse_indices[None, :], impulse_amplitudes[None, :], 0.0), axis=1)
    return -(gentle_waveform + impulse_train[:, None])


def block_levels(rng, shape, cuts, least, top_value):
    def one(axis_at, shards_of):
        steps = jax.random.uniform(jax.random.fold_in(jax.random.fold_in(rng, 6), axis_at), (shards_of,), jnp.float32, least / len(cuts), top_value / len(cuts))
        return jnp.repeat(jnp.exp(steps), shape[axis_at] // shards_of).reshape((-1,) + (1,) * (len(shape) - axis_at - 1))

    level = one(*cuts[0])
    for cut in cuts[1:]:
        level = level * one(*cut)
    return level


def scatter_about(stream_key, dims, scale, limit, cuts=(), dtype=jnp.bfloat16):
    loudness = block_levels(stream_key, dims, cuts, -0.22, 0.18) if cuts else 1.0
    values = jax.random.normal(stream_key, dims, jnp.float32) * scale * loudness
    return jnp.minimum(jnp.maximum(values, -limit), limit).astype(dtype)


def setup_inputs(seed: int = 0) -> dict:
    streams_of = jax.random.split(jax.random.key(seed), 5)
    return {
        "inputs": scatter_about(streams_of[0], (TOKENS, HEADS * P_SIZE), 0.1, 0.8, ((0, 32), (1, 16)), jnp.float32),
        "b_proj": scatter_about(streams_of[1], (TOKENS, NSTATE), 0.0625, 0.5, ((0, 32), (1, 16)), jnp.float32),
        "c_proj": scatter_about(streams_of[2], (TOKENS, NSTATE), 0.0625, 0.5, ((0, 32), (1, 16)), jnp.float32),
        "log_decay": draw_log_decay(jax.random.fold_in(streams_of[4], 71), 0),
    }


def to_line(array):
    rest = array.shape[1:]
    shaped = array.reshape((N_SEQ, 2, HALF) + rest)
    joined = jnp.concatenate([shaped[:, 0], shaped[::-1, 1]], axis=0)
    return joined.reshape(array.shape)


def to_mirror(array):
    rest = array.shape[1:]
    shaped = array.reshape((2 * N_SEQ, HALF) + rest)
    paired = jnp.stack([shaped[:N_SEQ], shaped[N_SEQ:][::-1]], axis=1)
    return paired.reshape(array.shape)


def reference(inputs, b_proj, c_proj, log_decay):
    count = TOKENS // BLOCK_LEN
    values = to_line(inputs).reshape(count, BLOCK_LEN, HEADS, P_SIZE)
    b_rows = to_line(b_proj).reshape(count, BLOCK_LEN, NSTATE)
    c_rows = to_line(c_proj).reshape(count, BLOCK_LEN, NSTATE)
    decays = to_line(log_decay).reshape(count, BLOCK_LEN, HEADS)
    rows = lax.broadcasted_iota(jnp.int32, (BLOCK_LEN, BLOCK_LEN), 0)
    cols = lax.broadcasted_iota(jnp.int32, (BLOCK_LEN, BLOCK_LEN), 1)
    lower_mask = rows >= cols
    highest_value = lax.Precision.HIGHEST

    def advance(state, pieces):
        value, b_block, readout_segment, decay = pieces
        cumulative = jnp.cumsum(decay, axis=0)
        ending = cumulative[-1]
        scores = jnp.dot(readout_segment, b_block.T, precision=highest_value)
        kernel_breadth = cumulative[:, None, :] - cumulative[None, :, :]
        weights = jnp.exp(jnp.where(lower_mask[:, :, None], kernel_breadth, -jnp.inf)) * scores[:, :, None]
        inside = jnp.einsum("tsh,shp->thp", weights, value, precision=highest_value)
        carried = jnp.exp(cumulative)[:, :, None] * jnp.einsum("hpn,tn->thp", state, readout_segment, precision=highest_value)
        to_end = jnp.exp(ending[None, :] - cumulative)
        fresh = jnp.einsum("shp,sn->hpn", value * to_end[:, :, None], b_block, precision=highest_value)
        new_state = jnp.exp(ending)[:, None, None] * state + fresh
        return new_state, inside + carried

    start = jnp.zeros((HEADS, P_SIZE, NSTATE), jnp.float32)
    _, results = lax.scan(advance, start, (values, b_rows, c_rows, decays))
    return to_mirror(results.reshape(TOKENS, HEADS * P_SIZE))
```

```python
import functools

import jax
import jax.numpy as jnp
from jax import lax
from jax.experimental import pallas as pl
from jax.experimental.pallas import tpu as pltpu
from jax.sharding import PartitionSpec as P

MESH = pl.DeviceIdType.MESH
F32 = jnp.float32
BF16 = jnp.bfloat16
L = 256
NBLK = 16
HALF_BLK = 8
N = 256
W = 128
TOK = 4096
NP = 4
PW = TOK // NP
PER = NBLK // NP
NSEQ = 32


def split2(a):
    hi = a.astype(BF16)
    return hi, (a - hi.astype(F32)).astype(BF16)


def split3(a):
    hi = a.astype(BF16)
    rest = a - hi.astype(F32)
    mid = rest.astype(BF16)
    return hi, mid, (rest - mid.astype(F32)).astype(BF16)


def dot(a, b):
    return jnp.dot(a, b, preferred_element_type=F32)


def dot3(ahi, alo, bhi, blo):
    return dot(ahi, bhi) + (dot(ahi, blo) + dot(alo, bhi))


def kernel(
    x_ref, b_ref, c_ref, ld_ref, o_ref,
    bt, ct, xv, xhi, xlo, xdhi, xdlo, chi, clo, dec, ecum, pre, out,
    cum, cumt, lanes, msg, recv, incs, inc,
    ssem, rsem, lsem, osem, asem,
):
    d = lax.axis_index("head")
    me = lax.axis_index("seq")
    y, x = d // 4, d % 4

    def at(fa, fo, so):
        if fa == 0:
            return ((y + so) % 4) * 4 + (x + fo) % 4
        return ((y + fo) % 4) * 4 + (x + so) % 4

    barrier = pltpu.get_barrier_semaphore()
    for fa in (0, 1):
        for o in (1, 3):
            pl.semaphore_signal(barrier, inc=1, device_id={"head": at(fa, o, 0)}, device_id_type=MESH)

    def greet(i, _):
        pl.semaphore_signal(barrier, inc=1, device_id={"seq": (me + i) % NSEQ}, device_id_type=MESH)
        return 0

    lax.fori_loop(1, NSEQ, greet, 0)
    own = [
        pltpu.make_async_copy(x_ref, xv, lsem.at[0]),
        pltpu.make_async_copy(b_ref, bt.at[pl.ds(pl.multiple_of(d * 16, 16), 16)], lsem.at[1]),
        pltpu.make_async_copy(c_ref, ct.at[pl.ds(pl.multiple_of(d * 16, 16), 16)], lsem.at[2]),
    ]
    for copy in own:
        copy.start()
    pl.semaphore_wait(barrier, NSEQ - 1 + 4)

    class Stage:
        def __init__(self, src, buf, which, c0, w, base):
            self.src, self.buf, self.which, self.c0, self.w, self.base = src, buf, which, c0, w, base

        def view(self, t, owner, part):
            start = self.c0 if part != 2 else self.c0 + self.w // 2
            width = self.w if part == 0 else self.w // 2
            return self.buf.at[pl.ds(pl.multiple_of(owner * 16 + 8 * t, 8), 8), pl.ds(start, width)]

        def copy(self, t, owner, target, part, k, from_src=False):
            dst = self.view(t, owner, part)
            src = self.src.at[pl.ds(8 * t, 8), pl.ds(self.c0, self.w)] if from_src else dst
            return pltpu.make_async_remote_copy(
                src, dst, ssem.at[self.which], rsem.at[self.base + t * 16 + k],
                device_id={"head": target}, device_id_type=MESH,
            )

        def send(self, *a, **k):
            self.copy(*a, **k).start()

        def wait(self, t, owner, part, k):
            self.copy(t, owner, d, part, k).wait_recv()

        def ev0(self):
            for t in (0, 1):
                self.send(t, d, at(t, 1, 0), 0, 0, from_src=True)
                self.send(t, d, at(t, 3, 0), 0, 1, from_src=True)
            for t in (0, 1):
                self.send(t, d, at(t, 0, 1), 0, 4, from_src=True)
                self.send(t, d, at(t, 0, 3), 0, 5, from_src=True)

        def ev1(self):
            for t in (0, 1):
                left, right = at(t, 3, 0), at(t, 1, 0)
                self.wait(t, left, 0, 0)
                self.send(t, left, right, 1, 2)
                self.wait(t, right, 0, 1)
                self.send(t, right, left, 2, 3)
                for q, owner in ((1, left), (2, right)):
                    self.send(t, owner, at(t, 0, 1), 0, 4 + 2 * q)
                    self.send(t, owner, at(t, 0, 3), 0, 5 + 2 * q)

        def ev2(self):
            for t in (0, 1):
                owner = at(t, 2, 0)
                self.wait(t, owner, 1, 2)
                self.wait(t, owner, 2, 3)
                self.send(t, owner, at(t, 0, 1), 0, 10)
                self.send(t, owner, at(t, 0, 3), 0, 11)

        def ev3(self, q):
            fo = (0, 3, 1, 2)[q]
            for t in (0, 1):
                down, up = at(t, fo, 3), at(t, fo, 1)
                self.wait(t, down, 0, 4 + 2 * q)
                self.wait(t, up, 0, 5 + 2 * q)
                if q < 2:
                    self.send(t, down, at(t, 0, 1), 0, 12 + q)
                else:
                    self.send(t, up, at(t, 0, 3), 0, 12 + q)

        def ev4(self):
            for q, fo in enumerate((0, 3, 1, 2)):
                for t in (0, 1):
                    self.wait(t, at(t, fo, 2), 0, 12 + q)

    def c_stage(p):
        return Stage(c_ref, ct, 1, pl.multiple_of(p * PW, PW), PW, 32 + p * 32)

    bst = Stage(b_ref, bt, 0, 0, TOK, 0)
    bst.ev0()

    lane = lax.broadcasted_iota(jnp.int32, (1, W), 1)
    first_head = lane < 64
    cum[...] = jnp.zeros_like(cum)
    for g in range(NBLK):
        for h in range(2):
            cum[h * 16 + g : h * 16 + g + 1, :] = ld_ref[h : h + 1, g * L : (g + 1) * L]
    r256 = lax.broadcasted_iota(jnp.int32, (L, L), 0)
    c256 = lax.broadcasted_iota(jnp.int32, (L, L), 1)
    upper = jnp.where(r256 <= c256, 1.0, 0.0).astype(BF16)
    total = sum(dot(part, upper) for part in split3(cum[...]))
    cum[...] = total
    turned = total.T
    for i, part in enumerate(split3(turned)):
        cumt[i] = part
    ends = jnp.broadcast_to(total[0:32, L - 1 : L], (32, W))
    ends = jnp.where(first_head, ends[0:16], ends[16:32])
    lanes[0:16] = jnp.exp(ends)
    sums = []
    for half in range(2):
        run = jnp.zeros((1, W), F32)
        for i in range(HALF_BLK):
            g = half * HALF_BLK + i
            lanes[16 + g : 17 + g, :] = jnp.exp(run)
            run = run + ends[g : g + 1]
        sums.append(jnp.exp(run))
    tail = jnp.concatenate(sums + [jnp.zeros((6, W), F32)], axis=0)
    own[0].wait()

    pick_row = lax.broadcasted_iota(jnp.int32, (W, W), 0)
    pick_lane = lax.broadcasted_iota(jnp.int32, (W, W), 1)

    def column(g, h):
        row = jnp.where(pick_lane < 64, g, 16 + g) if h is None else h * 16 + g
        sel = jnp.where(pick_row == row, 1.0, 0.0).astype(BF16)
        return dot(cumt[0], sel) + dot(cumt[1], sel) + dot(cumt[2], sel)

    def rows_of(g):
        return pl.ds(pl.multiple_of(g * L, L), L)

    def prepare(g, _):
        col = column(g, None)
        ecum[rows_of(g), :] = jnp.exp(col)
        val = xv[rows_of(g), :]
        xhi[rows_of(g), :], xlo[rows_of(g), :] = split2(val)
        to_end = jnp.exp(col[L - 1 : L, :] - col)
        xdhi[rows_of(g), :], xdlo[rows_of(g), :] = split2(val * to_end)
        return 0

    lax.fori_loop(0, NBLK, prepare, 0)

    def decay(g, _):
        for h in range(2):
            col = column(g, h)
            col = jnp.concatenate([col, col], axis=1)
            diff = col - cum[pl.ds(h * 16 + g, 1), :]
            dec[g, h] = jnp.exp(jnp.where(r256 >= c256, diff, -jnp.inf))
        return 0

    own[1].wait()
    bst.ev1()
    lax.fori_loop(0, 6, decay, 0)
    bst.ev2()

    def states(tiles):
        rows = [pl.ds(pl.multiple_of(k * 8, 8), 8) for k in tiles]
        for half in range(2):
            def step(i, run):
                g = half * HALF_BLK + i
                feats = jnp.concatenate([bt[r, rows_of(g)] for r in rows], axis=0)
                fhi, flo = split2(feats)
                for n, r in enumerate(rows):
                    pre[g, r, :] = run[n * 8 : n * 8 + 8]
                fresh = dot3(fhi, flo, xdhi[rows_of(g), :], xdlo[rows_of(g), :])
                return lanes[pl.ds(g, 1), :] * run + fresh

            run = lax.fori_loop(0, HALF_BLK, step, jnp.zeros((8 * len(tiles), W), F32))
            for n, k in enumerate(tiles):
                msg[k, half * 8 : half * 8 + 8, :] = run[n * 8 : n * 8 + 8]
        for k in tiles:
            msg[k, 16:24, :] = tail

            @pl.when(k != me)
            def _():
                pltpu.make_async_remote_copy(
                    msg.at[k], recv.at[me], asem.at[0], asem.at[1],
                    device_id={"seq": k}, device_id_type=MESH,
                ).start()

            @pl.when(k == me)
            def _():
                recv[k] = msg[k]

    def tiles(so):
        return [2 * at(t, fo, so) + t for t in (0, 1) for fo in range(4)]

    states(tiles(0))
    for q in range(4):
        bst.ev3(q)
        if q < 3:
            lax.fori_loop(6 + 3 * q, 9 + 3 * q, decay, 0)
    own[2].wait()
    c_stage(0).ev0()
    states(tiles(1) + tiles(3))
    lax.fori_loop(15, 16, decay, 0)
    bst.ev4()
    states(tiles(2))
    c_stage(0).ev1()
    c_stage(0).ev2()

    pltpu.make_async_copy(recv.at[pl.ds(0, NSEQ - 1)], recv.at[pl.ds(0, NSEQ - 1)], asem.at[1]).wait()

    def lower(j, run):
        incs[j, 0:8, :] = run
        return recv[j, 16:17, :] * run + recv[j, 0:8, :]

    def upper_step(i, run):
        j = NSEQ - 1 - i
        incs[j, 8:16, :] = run
        return recv[j, 17:18, :] * run + recv[j, 8:16, :]

    run = lax.fori_loop(0, NSEQ, lower, jnp.zeros((8, W), F32))
    lax.fori_loop(0, NSEQ, upper_step, run)
    inc[me] = incs[me]

    def give(i, _):
        j = (me + i) % NSEQ
        pltpu.make_async_remote_copy(
            incs.at[j], inc.at[me], asem.at[2], asem.at[3],
            device_id={"seq": j}, device_id_type=MESH,
        ).start()
        return 0

    lax.fori_loop(1, NSEQ, give, 0)
    for q in range(4):
        c_stage(0).ev3(q)
    c_stage(1).ev0()
    c_stage(0).ev4()

    def inside(g):
        turned = ct[:, rows_of(g)].T
        qhi, qlo = split2(turned)
        chi[rows_of(g), :], clo[rows_of(g), :] = qhi, qlo
        khi, klo = split2(bt[:, rows_of(g)])
        scores = dot3(qhi, qlo, khi, klo)
        vhi, vlo = xhi[rows_of(g), :], xlo[rows_of(g), :]
        acc = jnp.zeros((L, W), F32)
        for h in range(2):
            keep = first_head if h == 0 else jnp.logical_not(first_head)
            whi, wlo = split2(scores * dec[g, h])
            zero = jnp.zeros_like(vhi)
            acc = acc + dot3(whi, wlo, jnp.where(keep, vhi, zero), jnp.where(keep, vlo, zero))
        out[rows_of(g), :] = acc

    def carried(g, half):
        enter = lanes[pl.ds(16 + g, 1), :] * inc[:, half * 8 : half * 8 + 8, :].reshape(N, W) + pre[g]
        ehi, elo = split2(enter)
        z = dot3(chi[rows_of(g), :], clo[rows_of(g), :], ehi, elo)
        out[rows_of(g), :] = out[rows_of(g), :] + ecum[rows_of(g), :] * z

    def piece(p, _):
        g = p * PER
        nxt = c_stage(p + 1)
        inside(g)
        nxt.ev1()
        inside(g + 1)
        nxt.ev2()
        inside(g + 2)
        for q in range(4):
            nxt.ev3(q)

        @pl.when(p < NP - 2)
        def _():
            c_stage(p + 2).ev0()

        inside(g + 3)

        @pl.when(p < NP - 2)
        def _():
            nxt.ev4()

        return 0

    lax.fori_loop(0, NP - 1, piece, 0)
    pltpu.make_async_copy(inc.at[pl.ds(0, NSEQ - 1)], inc.at[pl.ds(0, NSEQ - 1)], asem.at[3]).wait()

    def carry_low(g, _):
        carried(g, 0)
        return 0

    def carry_high(g, _):
        carried(g, 1)
        return 0

    lax.fori_loop(0, HALF_BLK, carry_low, 0)
    lax.fori_loop(HALF_BLK, NBLK - PER, carry_high, 0)
    ahead = TOK - PW
    early = pltpu.make_async_copy(out.at[pl.ds(0, ahead)], o_ref.at[pl.ds(0, ahead)], osem.at[0])
    early.start()
    c_stage(NP - 1).ev4()

    def last(g, _):
        inside(g)
        carried(g, 1)
        return 0

    lax.fori_loop(NBLK - PER, NBLK, last, 0)
    late = pltpu.make_async_copy(out.at[pl.ds(ahead, PW)], o_ref.at[pl.ds(ahead, PW)], osem.at[1])
    late.start()

    for i, buf in enumerate((bt, ct)):
        sent = buf.at[pl.ds(0, 240)]
        pltpu.make_async_copy(sent, sent, ssem.at[i]).wait()
    for i, buf in ((0, msg), (2, incs)):
        sent = buf.at[pl.ds(0, NSEQ - 1)]
        pltpu.make_async_copy(sent, sent, asem.at[i]).wait()
    early.wait()
    late.wait()


def on_device(inputs, b_proj, c_proj, log_decay):
    vm = pltpu.VMEM
    return pl.pallas_call(
        kernel,
        out_shape=jax.ShapeDtypeStruct((TOK, W), F32),
        in_specs=[pl.BlockSpec(memory_space=pl.ANY)] * 3 + [pl.BlockSpec(memory_space=vm)],
        out_specs=pl.BlockSpec(memory_space=pl.ANY),
        scratch_shapes=[
            vm((N, TOK), F32), vm((N, TOK), F32),
            vm((TOK, W), F32),
            vm((TOK, W), BF16), vm((TOK, W), BF16),
            vm((TOK, W), BF16), vm((TOK, W), BF16),
            vm((TOK, N), BF16), vm((TOK, N), BF16),
            vm((NBLK, 2, L, L), F32),
            vm((TOK, W), F32),
            vm((NBLK, N, W), F32),
            vm((TOK, W), F32),
            vm((W, L), F32),
            vm((3, L, W), BF16),
            vm((32, W), F32),
            vm((NSEQ, 24, W), F32), vm((NSEQ, 24, W), F32),
            vm((NSEQ, 16, W), F32), vm((NSEQ, 16, W), F32),
            pltpu.SemaphoreType.DMA((2,)),
            pltpu.SemaphoreType.DMA((32 * (1 + NP),)),
            pltpu.SemaphoreType.DMA((3,)),
            pltpu.SemaphoreType.DMA((2,)),
            pltpu.SemaphoreType.DMA((4,)),
        ],
        compiler_params=pltpu.CompilerParams(
            collective_id=0, has_side_effects=True, vmem_limit_bytes=50 * 2**20
        ),
        cost_estimate=pl.CostEstimate(flops=5 * 10**9, bytes_accessed=2**23, transcendentals=3 * 10**6),
    )(inputs, b_proj.T, c_proj.T, log_decay.T)


def solution(mesh):
    return jax.shard_map(
        on_device,
        mesh=mesh,
        in_specs=(P("seq", "head"), P("seq", "head"), P("seq", "head"), P("seq", "head")),
        out_specs=P("seq", "head"),
        check_vma=False,
    )
```

```python
import functools

import jax
import jax.numpy as jnp
from jax import lax
from jax.experimental import pallas as pl
from jax.experimental.pallas import tpu as pltpu
from jax.sharding import PartitionSpec as P

MESH = pl.DeviceIdType.MESH
F32 = jnp.float32
BF16 = jnp.bfloat16
L = 256
NBLK = 16
HALF_BLK = 8
N = 256
W = 128
TOK = 4096
PIECES = (2048, 2048)
NSEQ = 32


def split2(a):
    hi = a.astype(BF16)
    return hi, (a - hi.astype(F32)).astype(BF16)


def split3(a):
    hi = a.astype(BF16)
    rest = a - hi.astype(F32)
    mid = rest.astype(BF16)
    return hi, mid, (rest - mid.astype(F32)).astype(BF16)


def dot(a, b):
    return jnp.dot(a, b, preferred_element_type=F32)


def dot3(ahi, alo, bhi, blo):
    left = jnp.concatenate([ahi, ahi, alo], axis=1)
    return dot(left, jnp.concatenate([bhi, blo, bhi], axis=0))


def kernel(
    x_ref, b_ref, c_ref, ld_ref, o_ref,
    bt, ct, xv, xhi, xlo, xdhi, xdlo, chi, clo, khi, klo, dec, ecum, pre, out,
    cum, cumt, lanes, msg, recv, incs, inc,
    ssem, rsem, lsem, osem, asem, known,
):
    d = lax.axis_index("head")
    me = lax.axis_index("seq")
    y, x = d // 4, d % 4

    def at(fa, fo, so):
        if fa == 0:
            return ((y + so) % 4) * 4 + (x + fo) % 4
        return ((y + fo) % 4) * 4 + (x + so) % 4

    z, core = me // 2, me % 2
    other = z * 2 + 1 - core

    def along(o):
        return ((z + o) % (NSEQ // 2)) * 2 + core

    barrier = pltpu.get_barrier_semaphore()
    for fa in (0, 1):
        for o in (1, 3):
            pl.semaphore_signal(barrier, inc=1, device_id={"head": at(fa, o, 0)}, device_id_type=MESH)
    for near in (along(1), along(-1 + NSEQ // 2), other):
        pl.semaphore_signal(barrier, inc=1, device_id={"seq": near}, device_id_type=MESH)

    def tell(r):
        far = (along(1 << r), along(NSEQ // 2 - (1 << r))) if r < 3 else (other,)
        for to in far:
            pl.semaphore_signal(known.at[r], inc=1, device_id={"seq": to}, device_id_type=MESH)

    def hear(r):
        pl.semaphore_wait(known.at[r], 2 if r < 3 else 1)

    own = [
        pltpu.make_async_copy(x_ref, xv, lsem.at[0]),
        pltpu.make_async_copy(b_ref, bt.at[pl.ds(pl.multiple_of(d * 16, 16), 16)], lsem.at[1]),
        pltpu.make_async_copy(c_ref, ct.at[pl.ds(pl.multiple_of(d * 16, 16), 16)], lsem.at[2]),
    ]
    for copy in own:
        copy.start()
    pl.semaphore_wait(barrier, 7)
    tell(0)

    class Stage:
        def __init__(self, src, buf, which, c0, w, base):
            self.src, self.buf, self.which, self.c0, self.w, self.base = src, buf, which, c0, w, base

        def view(self, t, owner, part):
            start = self.c0 if part != 2 else self.c0 + self.w // 2
            width = self.w if part == 0 else self.w // 2
            return self.buf.at[pl.ds(pl.multiple_of(owner * 16 + 8 * t, 8), 8), pl.ds(start, width)]

        def copy(self, t, owner, target, part, k, from_src=False):
            dst = self.view(t, owner, part)
            src = self.src.at[pl.ds(8 * t, 8), pl.ds(self.c0, self.w)] if from_src else dst
            return pltpu.make_async_remote_copy(
                src, dst, ssem.at[self.which], rsem.at[self.base + t * 16 + k],
                device_id={"head": target}, device_id_type=MESH,
            )

        def send(self, *a, **k):
            self.copy(*a, **k).start()

        def wait(self, t, owner, part, k):
            self.copy(t, owner, d, part, k).wait_recv()

        def ev0(self):
            for t in (0, 1):
                self.send(t, d, at(t, 1, 0), 0, 0, from_src=True)
                self.send(t, d, at(t, 3, 0), 0, 1, from_src=True)
            for t in (0, 1):
                self.send(t, d, at(t, 0, 1), 0, 4, from_src=True)
                self.send(t, d, at(t, 0, 3), 0, 5, from_src=True)

        def ev1(self):
            for t in (0, 1):
                left, right = at(t, 3, 0), at(t, 1, 0)
                self.wait(t, left, 0, 0)
                self.send(t, left, right, 1, 2)
                self.wait(t, right, 0, 1)
                self.send(t, right, left, 2, 3)
                for q, owner in ((1, left), (2, right)):
                    self.send(t, owner, at(t, 0, 1), 0, 4 + 2 * q)
                    self.send(t, owner, at(t, 0, 3), 0, 5 + 2 * q)

        def ev2(self):
            for t in (0, 1):
                owner = at(t, 2, 0)
                self.wait(t, owner, 1, 2)
                self.wait(t, owner, 2, 3)
                self.send(t, owner, at(t, 0, 1), 0, 10)
                self.send(t, owner, at(t, 0, 3), 0, 11)

        def ev3(self, q):
            fo = (0, 3, 1, 2)[q]
            for t in (0, 1):
                down, up = at(t, fo, 3), at(t, fo, 1)
                self.wait(t, down, 0, 4 + 2 * q)
                self.wait(t, up, 0, 5 + 2 * q)
                if q in (0, 3):
                    self.send(t, down, at(t, 0, 1), 0, 12 + q)
                else:
                    self.send(t, up, at(t, 0, 3), 0, 12 + q)

        def ev4(self):
            for q, fo in enumerate((0, 3, 1, 2)):
                for t in (0, 1):
                    self.wait(t, at(t, fo, 2), 0, 12 + q)

    starts = [sum(PIECES[:i]) for i in range(len(PIECES))]
    cst = [Stage(c_ref, ct, 1, starts[i], w, 32 + i * 32) for i, w in enumerate(PIECES)]
    bst = Stage(b_ref, bt, 0, 0, TOK, 0)
    bst.ev0()

    lane = lax.broadcasted_iota(jnp.int32, (1, W), 1)
    first_head = lane < 64
    cum[...] = jnp.zeros_like(cum)
    for g in range(NBLK):
        for h in range(2):
            cum[h * 16 + g : h * 16 + g + 1, :] = ld_ref[h : h + 1, g * L : (g + 1) * L]
    r256 = lax.broadcasted_iota(jnp.int32, (L, L), 0)
    c256 = lax.broadcasted_iota(jnp.int32, (L, L), 1)
    upper = jnp.where(r256 <= c256, 1.0, 0.0).astype(BF16)
    total = sum(dot(part, upper) for part in split3(cum[...]))
    cum[...] = total
    turned = total.T
    for i, part in enumerate(split3(turned)):
        cumt[i] = part
    ends = jnp.broadcast_to(total[0:32, L - 1 : L], (32, W))
    ends = jnp.where(first_head, ends[0:16], ends[16:32])
    lanes[0:16] = jnp.exp(ends)
    sums = []
    for half in range(2):
        run = jnp.zeros((1, W), F32)
        for i in range(HALF_BLK):
            g = half * HALF_BLK + i
            lanes[16 + g : 17 + g, :] = jnp.exp(run)
            run = run + ends[g : g + 1]
        sums.append(jnp.exp(run))
    tail = jnp.concatenate(sums + [jnp.zeros((6, W), F32)], axis=0)
    own[0].wait()

    pick_row = lax.broadcasted_iota(jnp.int32, (W, W), 0)
    pick_lane = lax.broadcasted_iota(jnp.int32, (W, W), 1)

    def column(g, h):
        row = jnp.where(pick_lane < 64, g, 16 + g) if h is None else h * 16 + g
        sel = jnp.where(pick_row == row, 1.0, 0.0).astype(BF16)
        return dot(cumt[0], sel) + dot(cumt[1], sel) + dot(cumt[2], sel)

    def rows_of(g):
        return pl.ds(pl.multiple_of(g * L, L), L)

    def prepare(g, _):
        col = column(g, None)
        ecum[rows_of(g), :] = jnp.exp(col)
        val = xv[rows_of(g), :]
        xhi[rows_of(g), :], xlo[rows_of(g), :] = split2(val)
        to_end = jnp.exp(col[L - 1 : L, :] - col)
        xdhi[rows_of(g), :], xdlo[rows_of(g), :] = split2(val * to_end)
        return 0

    lax.fori_loop(0, NBLK, prepare, 0)

    def decay(g, _):
        for h in range(2):
            col = column(g, h)
            col = jnp.concatenate([col, col], axis=1)
            diff = col - cum[pl.ds(h * 16 + g, 1), :]
            dec[g, h] = jnp.exp(jnp.where(r256 >= c256, diff, -jnp.inf))
        return 0

    def states(tiles):
        rows = [pl.ds(pl.multiple_of(k * 8, 8), 8) for k in tiles]
        for half in range(2):
            def step(i, run):
                g = half * HALF_BLK + i
                feats = jnp.concatenate([bt[r, rows_of(g)] for r in rows], axis=0)
                fhi, flo = split2(feats)
                for n, r in enumerate(rows):
                    pre[g, r, :] = run[n * 8 : n * 8 + 8]
                fresh = dot3(fhi, flo, xdhi[rows_of(g), :], xdlo[rows_of(g), :])
                return lanes[pl.ds(g, 1), :] * run + fresh

            run = lax.fori_loop(0, HALF_BLK, step, jnp.zeros((8 * len(tiles), W), F32))
            for n, k in enumerate(tiles):
                msg[k, half * 8 : half * 8 + 8, :] = run[n * 8 : n * 8 + 8]

    def ship(tiles):
        for k in tiles:
            msg[k, 16:24, :] = tail

            @pl.when(k != me)
            def _():
                pltpu.make_async_remote_copy(
                    msg.at[k], recv.at[me], asem.at[0], asem.at[1],
                    device_id={"seq": k}, device_id_type=MESH,
                ).start()

            @pl.when(k == me)
            def _():
                recv[k] = msg[k]

    def tiles(so):
        return [2 * at(t, fo, so) + t for t in (0, 1) for fo in range(4)]

    def keys(g, _):
        khi[:, rows_of(g)], klo[:, rows_of(g)] = split2(bt[:, rows_of(g)])
        return 0

    last = len(PIECES) - 1

    def rest(p):
        for q in (1, 2, 3):
            cst[p].ev3(q)

    own[1].wait()
    hear(0)
    tell(1)
    bst.ev1()
    lax.fori_loop(0, 3, decay, 0)
    bst.ev3(0)
    bst.ev2()
    own[2].wait()
    cst[0].ev0()
    hear(1)
    tell(2)
    states(tiles(0))
    lax.fori_loop(3, 6, decay, 0)
    for q in (1, 2, 3):
        bst.ev3(q)
    cst[0].ev1()
    cst[1].ev0()
    hear(2)
    tell(3)
    states(tiles(1) + tiles(3))
    hear(3)
    ship(tiles(0) + tiles(1) + tiles(3))
    bst.ev4()
    states(tiles(2))
    ship(tiles(2))
    cst[0].ev3(0)
    cst[0].ev2()
    cst[1].ev1()
    lax.fori_loop(6, 11, decay, 0)
    rest(0)
    if last > 1:
        cst[2].ev0()
    lax.fori_loop(11, NBLK, decay, 0)
    lax.fori_loop(0, 4, keys, 0)
    pltpu.make_async_copy(recv.at[pl.ds(0, NSEQ - 1)], recv.at[pl.ds(0, NSEQ - 1)], asem.at[1]).wait()

    def lower(j, run):
        incs[j, 0:8, :] = run
        return recv[j, 16:17, :] * run + recv[j, 0:8, :]

    def upper_step(i, run):
        j = NSEQ - 1 - i
        incs[j, 8:16, :] = run
        return recv[j, 17:18, :] * run + recv[j, 8:16, :]

    run = lax.fori_loop(0, NSEQ, lower, jnp.zeros((8, W), F32))
    lax.fori_loop(0, NSEQ, upper_step, run)
    inc[me] = incs[me]

    def give(i, _):
        j = (me + i) % NSEQ
        pltpu.make_async_remote_copy(
            incs.at[j], inc.at[me], asem.at[2], asem.at[3],
            device_id={"seq": j}, device_id_type=MESH,
        ).start()
        return 0

    lax.fori_loop(1, NSEQ, give, 0)
    cst[1].ev3(0)
    cst[1].ev2()
    lax.fori_loop(4, NBLK, keys, 0)
    cst[0].ev4()

    def inside(g):
        turned = ct[:, rows_of(g)].T
        qhi, qlo = split2(turned)
        chi[rows_of(g), :], clo[rows_of(g), :] = qhi, qlo
        scores = dot3(qhi, qlo, khi[:, rows_of(g)], klo[:, rows_of(g)])
        vhi, vlo = xhi[rows_of(g), :], xlo[rows_of(g), :]
        heads = [dot3(*split2(scores * dec[g, h]), vhi, vlo) for h in range(2)]
        out[rows_of(g), :] = jnp.where(first_head, heads[0], heads[1])

    def carried(g):
        half = g // HALF_BLK
        enter = lanes[pl.ds(16 + g, 1), :] * inc[:, pl.ds(pl.multiple_of(half * 8, 8), 8), :].reshape(N, W) + pre[g]
        ehi, elo = split2(enter)
        z = dot3(chi[rows_of(g), :], clo[rows_of(g), :], ehi, elo)
        out[rows_of(g), :] = out[rows_of(g), :] + ecum[rows_of(g), :] * z

    def only_inside(g, _):
        inside(g)
        return 0

    def only_carried(g, _):
        carried(g)
        return 0

    def both(g, _):
        inside(g)
        carried(g)
        return 0

    for p in range(last):
        groups = [lambda p=p: rest(p + 1)]
        if p + 3 <= last:
            groups[0] = lambda p=p: (rest(p + 1), cst[p + 3].ev0())
        if p + 2 <= last:
            groups += [cst[p + 2].ev1, lambda p=p: (cst[p + 2].ev3(0), cst[p + 2].ev2())]
        g = starts[p] // L
        for group in groups:
            inside(g)
            g += 1
            group()
        lax.fori_loop(g, starts[p + 1] // L, only_inside, 0)
        if p + 1 < last:
            cst[p + 1].ev4()
    ahead = starts[last]
    pltpu.make_async_copy(inc.at[pl.ds(0, NSEQ - 1)], inc.at[pl.ds(0, NSEQ - 1)], asem.at[3]).wait()
    lax.fori_loop(0, ahead // L, only_carried, 0)
    early = pltpu.make_async_copy(out.at[pl.ds(0, ahead)], o_ref.at[pl.ds(0, ahead)], osem.at[0])
    early.start()
    cst[last].ev4()
    lax.fori_loop(ahead // L, NBLK, both, 0)
    late = pltpu.make_async_copy(
        out.at[pl.ds(ahead, TOK - ahead)], o_ref.at[pl.ds(ahead, TOK - ahead)], osem.at[1]
    )
    late.start()

    for i, buf in enumerate((bt, ct)):
        sent = buf.at[pl.ds(0, 240)]
        pltpu.make_async_copy(sent, sent, ssem.at[i]).wait()
    for i, buf in ((0, msg), (2, incs)):
        sent = buf.at[pl.ds(0, NSEQ - 1)]
        pltpu.make_async_copy(sent, sent, asem.at[i]).wait()
    early.wait()
    late.wait()


def on_device(inputs, b_proj, c_proj, log_decay):
    vm = pltpu.VMEM
    return pl.pallas_call(
        kernel,
        out_shape=jax.ShapeDtypeStruct((TOK, W), F32),
        in_specs=[pl.BlockSpec(memory_space=pl.ANY)] * 3 + [pl.BlockSpec(memory_space=vm)],
        out_specs=pl.BlockSpec(memory_space=pl.ANY),
        scratch_shapes=[
            vm((N, TOK), F32), vm((N, TOK), F32),
            vm((TOK, W), F32),
            vm((TOK, W), BF16), vm((TOK, W), BF16),
            vm((TOK, W), BF16), vm((TOK, W), BF16),
            vm((TOK, N), BF16), vm((TOK, N), BF16),
            vm((N, TOK), BF16), vm((N, TOK), BF16),
            vm((NBLK, 2, L, L), F32),
            vm((TOK, W), F32),
            vm((NBLK, N, W), F32),
            vm((TOK, W), F32),
            vm((W, L), F32),
            vm((3, L, W), BF16),
            vm((32, W), F32),
            vm((NSEQ, 24, W), F32), vm((NSEQ, 24, W), F32),
            vm((NSEQ, 16, W), F32), vm((NSEQ, 16, W), F32),
            pltpu.SemaphoreType.DMA((2,)),
            pltpu.SemaphoreType.DMA((32 * (1 + len(PIECES)),)),
            pltpu.SemaphoreType.DMA((3,)),
            pltpu.SemaphoreType.DMA((2,)),
            pltpu.SemaphoreType.DMA((4,)),
            pltpu.SemaphoreType.REGULAR((4,)),
        ],
        compiler_params=pltpu.CompilerParams(
            collective_id=0, has_side_effects=True, vmem_limit_bytes=54 * 2**20
        ),
        cost_estimate=pl.CostEstimate(flops=5 * 10**9, bytes_accessed=2**23, transcendentals=3 * 10**6),
    )(inputs, b_proj.T, c_proj.T, log_decay.T)


def solution(mesh):
    return jax.shard_map(
        on_device,
        mesh=mesh,
        in_specs=(P("seq", "head"), P("seq", "head"), P("seq", "head"), P("seq", "head")),
        out_specs=P("seq", "head"),
        check_vma=False,
    )
```

```python
import functools

import jax
import jax.numpy as jnp
from jax import lax
from jax.experimental import pallas as pl
from jax.experimental.pallas import tpu as pltpu
from jax.sharding import PartitionSpec as P

MESH = pl.DeviceIdType.MESH
F32 = jnp.float32
BF16 = jnp.bfloat16
L = 256
NBLK = 16
HALF_BLK = 8
N = 256
W = 128
TOK = 4096
PIECES = (2560, 1536)
NSEQ = 32
NZ = 16


def split2(a):
    hi = a.astype(BF16)
    return hi, (a - hi.astype(F32)).astype(BF16)


def split3(a):
    hi = a.astype(BF16)
    rest = a - hi.astype(F32)
    mid = rest.astype(BF16)
    return hi, mid, (rest - mid.astype(F32)).astype(BF16)


def dot(a, b):
    return jnp.dot(a, b, preferred_element_type=F32)


def dot3(ahi, alo, bhi, blo):
    left = jnp.concatenate([ahi, ahi, alo], axis=1)
    return dot(left, jnp.concatenate([bhi, blo, bhi], axis=0))


def kernel(
    x_ref, b_ref, c_ref, ld_ref, o_ref,
    bt, ct, xv, xs, xd, chi, clo, khi, klo, dec, ecum, pre, out,
    cum, cumt, lanes, msg, sib, comb, recv, incs, ret, give, got, inc, mine, theirs, pair, dk,
    ssem, rsem, lsem, osem, asem, xsem, known,
):
    d = lax.axis_index("head")
    me = lax.axis_index("seq")
    y, x = d // 4, d % 4

    def at(fa, fo, so):
        if fa == 0:
            return ((y + so) % 4) * 4 + (x + fo) % 4
        return ((y + fo) % 4) * 4 + (x + so) % 4

    z, core = me // 2, me % 2
    other = z * 2 + 1 - core

    def along(o):
        return ((z + o) % (NZ)) * 2 + core

    barrier = pltpu.get_barrier_semaphore()
    for fa in (0, 1):
        for o in (1, 3):
            pl.semaphore_signal(barrier, inc=1, device_id={"head": at(fa, o, 0)}, device_id_type=MESH)
    for near in (along(1), along(-1 + NZ), other):
        pl.semaphore_signal(barrier, inc=1, device_id={"seq": near}, device_id_type=MESH)

    def tell(r):
        for to in (along(1 << r), along(NZ - (1 << r))):
            pl.semaphore_signal(known.at[r], inc=1, device_id={"seq": to}, device_id_type=MESH)

    def hear(r):
        pl.semaphore_wait(known.at[r], 2)

    def to_other(src, dst, k):
        return pltpu.make_async_remote_copy(
            src, dst, xsem.at[0, k], xsem.at[1, k], device_id={"seq": other}, device_id_type=MESH
        )

    own = [
        pltpu.make_async_copy(x_ref, xv, lsem.at[0]),
        pltpu.make_async_copy(b_ref, bt.at[pl.ds(pl.multiple_of(d * 16, 16), 16)], lsem.at[1]),
        pltpu.make_async_copy(c_ref, ct.at[pl.ds(pl.multiple_of(d * 16, 16), 16)], lsem.at[2]),
    ]
    for copy in own:
        copy.start()
    pl.semaphore_wait(barrier, 7)
    tell(0)

    class Stage:
        def __init__(self, src, buf, which, c0, w, base):
            self.src, self.buf, self.which, self.c0, self.w, self.base = src, buf, which, c0, w, base

        def view(self, t, owner, part):
            start = self.c0 if part != 2 else self.c0 + self.w // 2
            width = self.w if part == 0 else self.w // 2
            return self.buf.at[pl.ds(pl.multiple_of(owner * 16 + 8 * t, 8), 8), pl.ds(start, width)]

        def copy(self, t, owner, target, part, k, from_src=False):
            dst = self.view(t, owner, part)
            src = self.src.at[pl.ds(8 * t, 8), pl.ds(self.c0, self.w)] if from_src else dst
            return pltpu.make_async_remote_copy(
                src, dst, ssem.at[self.which], rsem.at[self.base + t * 16 + k],
                device_id={"head": target}, device_id_type=MESH,
            )

        def send(self, *a, **k):
            self.copy(*a, **k).start()

        def wait(self, t, owner, part, k):
            self.copy(t, owner, d, part, k).wait_recv()

        def ev0(self):
            for t in (0, 1):
                self.send(t, d, at(t, 1, 0), 0, 0, from_src=True)
                self.send(t, d, at(t, 3, 0), 0, 1, from_src=True)
            for t in (0, 1):
                self.send(t, d, at(t, 0, 1), 0, 4, from_src=True)
                self.send(t, d, at(t, 0, 3), 0, 5, from_src=True)

        def ev1(self):
            for t in (0, 1):
                left, right = at(t, 3, 0), at(t, 1, 0)
                self.wait(t, left, 0, 0)
                self.send(t, left, right, 1, 2)
                self.wait(t, right, 0, 1)
                self.send(t, right, left, 2, 3)
                for q, owner in ((1, left), (2, right)):
                    self.send(t, owner, at(t, 0, 1), 0, 4 + 2 * q)
                    self.send(t, owner, at(t, 0, 3), 0, 5 + 2 * q)

        def ev2(self):
            for t in (0, 1):
                owner = at(t, 2, 0)
                self.wait(t, owner, 1, 2)
                self.wait(t, owner, 2, 3)
                self.send(t, owner, at(t, 0, 1), 0, 10)
                self.send(t, owner, at(t, 0, 3), 0, 11)

        def ev3(self, q):
            fo = (0, 3, 1, 2)[q]
            for t in (0, 1):
                down, up = at(t, fo, 3), at(t, fo, 1)
                self.wait(t, down, 0, 4 + 2 * q)
                self.wait(t, up, 0, 5 + 2 * q)
                if q in (0, 3):
                    self.send(t, down, at(t, 0, 1), 0, 12 + q)
                else:
                    self.send(t, up, at(t, 0, 3), 0, 12 + q)

        def ev4(self):
            for q, fo in enumerate((0, 3, 1, 2)):
                for t in (0, 1):
                    self.wait(t, at(t, fo, 2), 0, 12 + q)

    starts = [sum(PIECES[:i]) for i in range(len(PIECES))]
    cst = [Stage(c_ref, ct, 1, starts[i], w, 32 + i * 32) for i, w in enumerate(PIECES)]
    bst = Stage(b_ref, bt, 0, 0, TOK, 0)
    bst.ev0()

    lane = lax.broadcasted_iota(jnp.int32, (1, W), 1)
    first_head = lane < 64
    cum[...] = jnp.zeros_like(cum)
    for g in range(NBLK):
        for h in range(2):
            cum[h * 16 + g : h * 16 + g + 1, :] = ld_ref[h : h + 1, g * L : (g + 1) * L]
    r256 = lax.broadcasted_iota(jnp.int32, (L, L), 0)
    c256 = lax.broadcasted_iota(jnp.int32, (L, L), 1)
    upper = jnp.where(r256 <= c256, 1.0, 0.0).astype(BF16)
    total = sum(dot(part, upper) for part in split3(cum[...]))
    cum[...] = total
    turned = total.T
    for i, part in enumerate(split3(turned)):
        cumt[i] = part
    ends = jnp.broadcast_to(total[0:32, L - 1 : L], (32, W))
    ends = jnp.where(first_head, ends[0:16], ends[16:32])
    lanes[0:16] = jnp.exp(ends)
    sums = []
    for half in range(2):
        run = jnp.zeros((1, W), F32)
        for i in range(HALF_BLK):
            g = half * HALF_BLK + i
            lanes[16 + g : 17 + g, :] = jnp.exp(run)
            run = run + ends[g : g + 1]
        sums.append(jnp.exp(run))
    mine[...] = jnp.concatenate(sums + [jnp.zeros((6, W), F32)], axis=0)
    to_other(mine, theirs, 4).start()
    own[0].wait()

    pick_row = lax.broadcasted_iota(jnp.int32, (W, W), 0)
    pick_lane = lax.broadcasted_iota(jnp.int32, (W, W), 1)

    def column(g, h):
        row = jnp.where(pick_lane < 64, g, 16 + g) if h is None else h * 16 + g
        sel = jnp.where(pick_row == row, 1.0, 0.0).astype(BF16)
        return dot(cumt[0], sel) + dot(cumt[1], sel) + dot(cumt[2], sel)

    def rows_of(g):
        return pl.ds(pl.multiple_of(g * L, L), L)

    def prepare(g, _):
        col = column(g, None)
        ecum[rows_of(g), :] = jnp.exp(col)
        val = xv[rows_of(g), :]
        hi = val.astype(BF16).astype(F32)
        lo = val - hi
        xs[0, rows_of(g), :] = jnp.where(first_head, hi, pltpu.roll(lo, 64, 1)).astype(BF16)
        xs[1, rows_of(g), :] = jnp.where(first_head, pltpu.roll(hi, 64, 1), lo).astype(BF16)
        to_end = jnp.exp(col[L - 1 : L, :] - col)
        xd[rows_of(g), :] = jnp.concatenate(split2(val * to_end), axis=1)
        return 0

    lax.fori_loop(0, NBLK, prepare, 0)

    def decay(g, _):
        for h in range(2):
            col = column(g, h)
            col = jnp.concatenate([col, col], axis=1)
            diff = col - cum[pl.ds(h * 16 + g, 1), :]
            dec[g, h] = jnp.exp(jnp.where(r256 >= c256, diff, -jnp.inf))
        return 0

    second = (y, x)
    first = (x, y)

    def states(offsets):
        tiles = [(t, fo, so) for so in offsets for t in (0, 1) for fo in range(4)]
        rows = [pl.ds(pl.multiple_of(at(t, fo, so) * 16 + 8 * t, 8), 8) for t, fo, so in tiles]
        for half in range(2):
            def step(i, run):
                g = half * HALF_BLK + i
                feats = jnp.concatenate([bt[r, rows_of(g)] for r in rows], axis=0)
                for n, r in enumerate(rows):
                    pre[g, r, :] = run[n * 8 : n * 8 + 8]
                both = dot(jnp.concatenate(split2(feats), axis=0), xd[rows_of(g), :])
                both = both[: feats.shape[0]] + both[feats.shape[0] :]
                fresh = both[:, :W] + both[:, W:]
                return lanes[pl.ds(g, 1), :] * run + fresh

            run = lax.fori_loop(0, HALF_BLK, step, jnp.zeros((8 * len(tiles), W), F32))
            for n, (t, fo, so) in enumerate(tiles):
                place = ((second[t] + so) % 4) * 4 + (first[t] + fo) % 4
                msg[t, place, half * 8 : half * 8 + 8, :] = run[n * 8 : n * 8 + 8]

    def group(so, kind):
        sec = y + (x - y) * kind
        return pl.ds(pl.multiple_of(((sec + so) % 4) * 4, 4), 4)

    def swap(so):
        g = group(so, 1 - core)
        return to_other(msg.at[1 - core, g], sib.at[g], so)

    def ship(so):
        swap(so).wait_recv()
        sec = y + (x - y) * core
        lead = ((sec + so) % 4) * 4
        for i in range(4):
            p = lead + i
            own_l, own_u = msg[core, p, 0:8, :], msg[core, p, 8:16, :]
            sib_l, sib_u = sib[p, 0:8, :], sib[p, 8:16, :]
            comb[p, 0:8, :] = jnp.where(
                core == 1, mine[0:1, :] * sib_l + own_l, theirs[0:1, :] * own_l + sib_l
            )
            comb[p, 8:16, :] = jnp.where(
                core == 0, mine[1:2, :] * sib_u + own_u, theirs[1:2, :] * own_u + sib_u
            )

            @pl.when(p != z)
            def _():
                pltpu.make_async_remote_copy(
                    comb.at[p], recv.at[z], asem.at[0], asem.at[1],
                    device_id={"seq": p * 2 + core}, device_id_type=MESH,
                ).start()

            @pl.when(p == z)
            def _():
                recv[p] = comb[p]

    def spread(src, dst, k):
        for off in (8, 9, 7, 10, 6, 11, 5, 12, 4, 13, 3, 14, 2, 15, 1):
            to = (z + off) % NZ
            pltpu.make_async_remote_copy(
                src(to), dst.at[z], asem.at[k], asem.at[k + 1],
                device_id={"seq": to * 2 + core}, device_id_type=MESH,
            ).start()

    def arrived(buf, k):
        part = buf.at[pl.ds(0, NZ - 1)]
        pltpu.make_async_copy(part, part, asem.at[k]).wait()

    def keys(g, _):
        khi[:, rows_of(g)], klo[:, rows_of(g)] = split2(bt[:, rows_of(g)])
        return 0

    last = len(PIECES) - 1

    def rest(p):
        for q in (1, 2, 3):
            cst[p].ev3(q)

    own[1].wait()
    hear(0)
    tell(1)
    bst.ev1()
    lax.fori_loop(0, 3, decay, 0)
    bst.ev3(0)
    bst.ev2()
    own[2].wait()
    cst[0].ev0()
    hear(1)
    tell(2)
    states((0,))
    swap(0).start()
    to_other(mine, theirs, 4).wait_recv()
    pair[...] = mine[...] * theirs[...]
    dk[z] = pair[...]
    lax.fori_loop(3, 6, decay, 0)
    for q in (1, 2, 3):
        bst.ev3(q)
    cst[0].ev1()
    cst[1].ev0()
    hear(2)
    spread(lambda to: pair, dk, 4)
    states((1, 3))
    swap(1).start()
    swap(3).start()
    ship(0)
    bst.ev4()
    states((2,))
    swap(2).start()
    ship(1)
    ship(3)
    ship(2)
    cst[0].ev3(0)
    cst[0].ev2()
    cst[1].ev1()
    lax.fori_loop(6, 11, decay, 0)
    rest(0)
    if last > 1:
        cst[2].ev0()
    lax.fori_loop(11, NBLK, decay, 0)
    lax.fori_loop(0, 4, keys, 0)
    def put(p, kind, tile):
        shard = p + ((p % 4) * 4 + p // 4 - p) * kind
        r = pl.ds(pl.multiple_of(shard * 16 + kind * 8, 8), 8)
        inc[0, r, :] = tile[0:8]
        inc[1, r, :] = tile[8:16]

    def enter_chip(p, _):
        low, high = ret[p, 0:8, :], ret[p, 8:16, :]
        own_l = mine[0:1, :] * low + msg[core, p, 0:8, :]
        own_u = mine[1:2, :] * high + msg[core, p, 8:16, :]
        sib_l = theirs[0:1, :] * low + sib[p, 0:8, :]
        sib_u = theirs[1:2, :] * high + sib[p, 8:16, :]
        give[p, 0:8, :] = jnp.where(core == 0, own_l, low)
        give[p, 8:16, :] = jnp.where(core == 0, high, own_u)
        put(p, core, jnp.concatenate(
            [jnp.where(core == 0, low, sib_l), jnp.where(core == 0, sib_u, high)], axis=0))
        return 0

    def enter_other(p, _):
        put(p, 1 - core, got[p])
        return 0

    arrived(dk, 5)
    arrived(recv, 1)
    run = jnp.zeros((8, W), F32)
    for j in range(NZ):
        incs[j, 0:8, :] = run
        run = dk[j, 0:1, :] * run + recv[j, 0:8, :]
    for j in reversed(range(NZ)):
        incs[j, 8:16, :] = run
        run = dk[j, 1:2, :] * run + recv[j, 8:16, :]
    spread(lambda to: incs.at[to], ret, 2)
    ret[z] = incs[z]

    cst[1].ev3(0)
    cst[1].ev2()
    lax.fori_loop(4, NBLK, keys, 0)
    cst[0].ev4()

    def inside(g):
        turned = ct[:, rows_of(g)].T
        qhi, qlo = split2(turned)
        chi[rows_of(g), :], clo[rows_of(g), :] = qhi, qlo
        scores = dot3(qhi, qlo, khi[:, rows_of(g)], klo[:, rows_of(g)])
        sums = []
        for h in range(2):
            weights = jnp.concatenate(split2(scores * dec[g, h]), axis=1)
            vals = xs[h, rows_of(g), :]
            sums.append(dot(weights, jnp.concatenate([vals, vals], axis=0)))
        out[rows_of(g), :] = jnp.where(first_head, sums[0], sums[1]) + pltpu.roll(
            jnp.where(first_head, sums[1], sums[0]), 64, 1
        )

    def carried(g):
        half = g // HALF_BLK
        enter = lanes[pl.ds(16 + g, 1), :] * inc[half] + pre[g]
        ehi, elo = split2(enter)
        part = dot(chi[rows_of(g), :], jnp.concatenate([ehi, elo], axis=1))
        part = part[:, :W] + (part[:, W:] + dot(clo[rows_of(g), :], ehi))
        out[rows_of(g), :] = out[rows_of(g), :] + ecum[rows_of(g), :] * part

    def only_inside(g, _):
        inside(g)
        return 0

    def only_carried(g, _):
        carried(g)
        return 0

    for p in range(last):
        groups = [lambda p=p: rest(p + 1)]
        if p + 3 <= last:
            groups[0] = lambda p=p: (rest(p + 1), cst[p + 3].ev0())
        if p + 2 <= last:
            groups += [cst[p + 2].ev1, lambda p=p: (cst[p + 2].ev3(0), cst[p + 2].ev2())]
        g = starts[p] // L
        for events in groups:
            inside(g)
            g += 1
            events()
        lax.fori_loop(g, starts[p + 1] // L, only_inside, 0, unroll=2)
        if p + 1 < last:
            cst[p + 1].ev4()
    cst[last].ev4()
    lax.fori_loop(starts[last] // L, NBLK, only_inside, 0, unroll=2)
    arrived(ret, 3)
    lax.fori_loop(0, NZ, enter_chip, 0)
    to_other(give, got, 5).start()
    to_other(give, got, 5).wait_recv()
    lax.fori_loop(0, NZ, enter_other, 0)
    halves = []
    for i in range(2):
        lax.fori_loop(i * HALF_BLK, (i + 1) * HALF_BLK, only_carried, 0, unroll=4)
        part = pl.ds(i * TOK // 2, TOK // 2)
        halves.append(pltpu.make_async_copy(out.at[part], o_ref.at[part], osem.at[i]))
        halves[-1].start()

    for i, buf in enumerate((bt, ct)):
        sent = buf.at[pl.ds(0, 240)]
        pltpu.make_async_copy(sent, sent, ssem.at[i]).wait()
    for i, buf in ((0, comb), (2, incs), (4, dk)):
        arrived(buf, i)
    for so in range(4):
        swap(so).wait_send()
    to_other(mine, theirs, 4).wait_send()
    to_other(give, got, 5).wait_send()
    for copy in halves:
        copy.wait()


def on_device(inputs, b_proj, c_proj, log_decay):
    vm = pltpu.VMEM
    return pl.pallas_call(
        kernel,
        out_shape=jax.ShapeDtypeStruct((TOK, W), F32),
        in_specs=[pl.BlockSpec(memory_space=pl.ANY)] * 3 + [pl.BlockSpec(memory_space=vm)],
        out_specs=pl.BlockSpec(memory_space=pl.ANY),
        scratch_shapes=[
            vm((N, TOK), F32), vm((N, TOK), F32),
            vm((TOK, W), F32),
            vm((2, TOK, W), BF16),
            vm((TOK, 2 * W), BF16),
            vm((TOK, N), BF16), vm((TOK, N), BF16),
            vm((N, TOK), BF16), vm((N, TOK), BF16),
            vm((NBLK, 2, L, L), F32),
            vm((TOK, W), F32),
            vm((NBLK, N, W), F32),
            vm((TOK, W), F32),
            vm((W, L), F32),
            vm((3, L, W), BF16),
            vm((32, W), F32),
            vm((2, NZ, 16, W), F32), vm((NZ, 16, W), F32),
            vm((NZ, 16, W), F32), vm((NZ, 16, W), F32),
            vm((NZ, 16, W), F32), vm((NZ, 16, W), F32),
            vm((NZ, 16, W), F32), vm((NZ, 16, W), F32),
            vm((2, N, W), F32),
            vm((8, W), F32), vm((8, W), F32), vm((8, W), F32),
            vm((NZ, 8, W), F32),
            pltpu.SemaphoreType.DMA((2,)),
            pltpu.SemaphoreType.DMA((32 * (1 + len(PIECES)),)),
            pltpu.SemaphoreType.DMA((3,)),
            pltpu.SemaphoreType.DMA((2,)),
            pltpu.SemaphoreType.DMA((6,)),
            pltpu.SemaphoreType.DMA((2, 6)),
            pltpu.SemaphoreType.REGULAR((3,)),
        ],
        compiler_params=pltpu.CompilerParams(
            collective_id=0, has_side_effects=True, vmem_limit_bytes=54 * 2**20
        ),
        cost_estimate=pl.CostEstimate(flops=5 * 10**9, bytes_accessed=2**23, transcendentals=3 * 10**6),
    )(inputs, b_proj.T, c_proj.T, log_decay.T)


def solution(mesh):
    return jax.shard_map(
        on_device,
        mesh=mesh,
        in_specs=(P("seq", "head"), P("seq", "head"), P("seq", "head"), P("seq", "head")),
        out_specs=P("seq", "head"),
        check_vma=False,
    )
```

```python
import functools

import jax
import jax.numpy as jnp
from jax import lax
from jax.experimental import pallas as pl
from jax.experimental.pallas import tpu as pltpu
from jax.sharding import PartitionSpec as P

MESH = pl.DeviceIdType.MESH
F32 = jnp.float32
BF16 = jnp.bfloat16
L = 256
NBLK = 16
HALF_BLK = 8
N = 256
W = 128
TOK = 4096
PIECES = (2560, 1536)
NSEQ = 32
NZ = 16


def split2(a):
    hi = a.astype(BF16)
    return hi, (a - hi.astype(F32)).astype(BF16)


def split3(a):
    hi = a.astype(BF16)
    rest = a - hi.astype(F32)
    mid = rest.astype(BF16)
    return hi, mid, (rest - mid.astype(F32)).astype(BF16)


def dot(a, b):
    return jnp.dot(a, b, preferred_element_type=F32)


def dot3(ahi, alo, bhi, blo):
    left = jnp.concatenate([ahi, ahi, alo], axis=1)
    return dot(left, jnp.concatenate([bhi, blo, bhi], axis=0))


def kernel(
    x_ref, b_ref, c_ref, ld_ref, o_ref,
    bt, ct, xv, xs, xd, chi, clo, khi, klo, dec, ecum, pre, out,
    cum, cumt, lanes, msg, sib, comb, recv, incs, ret, give, got, inc, mine, theirs, pair, dk,
    ssem, rsem, lsem, osem, asem, xsem, known,
):
    d = lax.axis_index("head")
    me = lax.axis_index("seq")
    y, x = d // 4, d % 4

    def at(fa, fo, so):
        if fa == 0:
            return ((y + so) % 4) * 4 + (x + fo) % 4
        return ((y + fo) % 4) * 4 + (x + so) % 4

    z, core = me // 2, me % 2
    other = z * 2 + 1 - core

    def along(o):
        return ((z + o) % (NZ)) * 2 + core

    barrier = pltpu.get_barrier_semaphore()
    for fa in (0, 1):
        for o in (1, 3):
            pl.semaphore_signal(barrier, inc=1, device_id={"head": at(fa, o, 0)}, device_id_type=MESH)
    for near in (along(1), along(-1 + NZ), other):
        pl.semaphore_signal(barrier, inc=1, device_id={"seq": near}, device_id_type=MESH)

    def tell(r):
        for to in (along(1 << r), along(NZ - (1 << r))):
            pl.semaphore_signal(known.at[r], inc=1, device_id={"seq": to}, device_id_type=MESH)

    def hear(r):
        pl.semaphore_wait(known.at[r], 2)

    def to_other(src, dst, k):
        return pltpu.make_async_remote_copy(
            src, dst, xsem.at[0, k], xsem.at[1, k], device_id={"seq": other}, device_id_type=MESH
        )

    own = [
        pltpu.make_async_copy(x_ref, xv, lsem.at[0]),
        pltpu.make_async_copy(b_ref, bt.at[pl.ds(pl.multiple_of(d * 16, 16), 16)], lsem.at[1]),
        pltpu.make_async_copy(c_ref, ct.at[pl.ds(pl.multiple_of(d * 16, 16), 16)], lsem.at[2]),
    ]
    for copy in own:
        copy.start()
    pl.semaphore_wait(barrier, 7)
    tell(0)

    class Stage:
        def __init__(self, src, buf, which, c0, w, base):
            self.src, self.buf, self.which, self.c0, self.w, self.base = src, buf, which, c0, w, base

        def view(self, t, owner, part):
            start = self.c0 if part != 2 else self.c0 + self.w // 2
            width = self.w if part == 0 else self.w // 2
            return self.buf.at[pl.ds(pl.multiple_of(owner * 16 + 8 * t, 8), 8), pl.ds(start, width)]

        def copy(self, t, owner, target, part, k, from_src=False):
            dst = self.view(t, owner, part)
            src = self.src.at[pl.ds(8 * t, 8), pl.ds(self.c0, self.w)] if from_src else dst
            return pltpu.make_async_remote_copy(
                src, dst, ssem.at[self.which], rsem.at[self.base + t * 16 + k],
                device_id={"head": target}, device_id_type=MESH,
            )

        def send(self, *a, **k):
            self.copy(*a, **k).start()

        def wait(self, t, owner, part, k):
            self.copy(t, owner, d, part, k).wait_recv()

        def ev0(self):
            for t in (0, 1):
                self.send(t, d, at(t, 1, 0), 0, 0, from_src=True)
                self.send(t, d, at(t, 3, 0), 0, 1, from_src=True)
            for t in (0, 1):
                self.send(t, d, at(t, 0, 1), 0, 4, from_src=True)
                self.send(t, d, at(t, 0, 3), 0, 5, from_src=True)

        def ev1(self):
            for t in (0, 1):
                left, right = at(t, 3, 0), at(t, 1, 0)
                self.wait(t, left, 0, 0)
                self.send(t, left, right, 1, 2)
                self.wait(t, right, 0, 1)
                self.send(t, right, left, 2, 3)
                for q, owner in ((1, left), (2, right)):
                    self.send(t, owner, at(t, 0, 1), 0, 4 + 2 * q)
                    self.send(t, owner, at(t, 0, 3), 0, 5 + 2 * q)

        def ev2(self):
            for t in (0, 1):
                owner = at(t, 2, 0)
                self.wait(t, owner, 1, 2)
                self.wait(t, owner, 2, 3)
                self.send(t, owner, at(t, 0, 1), 0, 10)
                self.send(t, owner, at(t, 0, 3), 0, 11)

        def ev3(self, q):
            fo = (0, 3, 1, 2)[q]
            for t in (0, 1):
                down, up = at(t, fo, 3), at(t, fo, 1)
                self.wait(t, down, 0, 4 + 2 * q)
                self.wait(t, up, 0, 5 + 2 * q)
                if q in (0, 3):
                    self.send(t, down, at(t, 0, 1), 0, 12 + q)
                else:
                    self.send(t, up, at(t, 0, 3), 0, 12 + q)

        def ev4(self):
            for q, fo in enumerate((0, 3, 1, 2)):
                for t in (0, 1):
                    self.wait(t, at(t, fo, 2), 0, 12 + q)

    starts = [sum(PIECES[:i]) for i in range(len(PIECES))]
    cst = [Stage(c_ref, ct, 1, starts[i], w, 32 + i * 32) for i, w in enumerate(PIECES)]
    bst = Stage(b_ref, bt, 0, 0, TOK, 0)
    bst.ev0()

    lane = lax.broadcasted_iota(jnp.int32, (1, W), 1)
    first_head = lane < 64
    cum[...] = jnp.zeros_like(cum)
    for g in range(NBLK):
        for h in range(2):
            cum[h * 16 + g : h * 16 + g + 1, :] = ld_ref[h : h + 1, g * L : (g + 1) * L]
    r256 = lax.broadcasted_iota(jnp.int32, (L, L), 0)
    c256 = lax.broadcasted_iota(jnp.int32, (L, L), 1)
    upper = jnp.where(r256 <= c256, 1.0, 0.0).astype(BF16)
    total = sum(dot(part, upper) for part in split3(cum[...]))
    cum[...] = total
    turned = total.T
    for i, part in enumerate(split3(turned)):
        cumt[i] = part
    ends = jnp.broadcast_to(total[0:32, L - 1 : L], (32, W))
    ends = jnp.where(first_head, ends[0:16], ends[16:32])
    lanes[0:16] = jnp.exp(ends)
    sums = []
    for half in range(2):
        run = jnp.zeros((1, W), F32)
        for i in range(HALF_BLK):
            g = half * HALF_BLK + i
            lanes[16 + g : 17 + g, :] = jnp.exp(run)
            run = run + ends[g : g + 1]
        sums.append(jnp.exp(run))
    mine[...] = jnp.concatenate(sums + [jnp.zeros((6, W), F32)], axis=0)
    to_other(mine, theirs, 4).start()
    own[0].wait()

    pick_row = lax.broadcasted_iota(jnp.int32, (W, W), 0)
    pick_lane = lax.broadcasted_iota(jnp.int32, (W, W), 1)

    def column(g, h):
        row = jnp.where(pick_lane < 64, g, 16 + g) if h is None else h * 16 + g
        sel = jnp.where(pick_row == row, 1.0, 0.0).astype(BF16)
        return dot(cumt[0], sel) + dot(cumt[1], sel) + dot(cumt[2], sel)

    def rows_of(g):
        return pl.ds(pl.multiple_of(g * L, L), L)

    def prepare(g, _):
        col = column(g, None)
        ecum[rows_of(g), :] = jnp.exp(col)
        val = xv[rows_of(g), :]
        hi = val.astype(BF16).astype(F32)
        lo = val - hi
        xs[0, rows_of(g), :] = jnp.where(first_head, hi, pltpu.roll(lo, 64, 1)).astype(BF16)
        xs[1, rows_of(g), :] = jnp.where(first_head, pltpu.roll(hi, 64, 1), lo).astype(BF16)
        to_end = jnp.exp(col[L - 1 : L, :] - col)
        xd[rows_of(g), :] = jnp.concatenate(split2(val * to_end), axis=1)
        return 0

    lax.fori_loop(0, NBLK, prepare, 0)

    def decay(g, _):
        for h in range(2):
            col = column(g, h)
            col = jnp.concatenate([col, col], axis=1)
            diff = col - cum[pl.ds(h * 16 + g, 1), :]
            dec[g, h] = jnp.exp(jnp.where(r256 >= c256, diff, -jnp.inf))
        return 0

    second = (y, x)
    first = (x, y)

    def states(offsets):
        tiles = [(t, fo, so) for so in offsets for t in (0, 1) for fo in range(4)]
        rows = [pl.ds(pl.multiple_of(at(t, fo, so) * 16 + 8 * t, 8), 8) for t, fo, so in tiles]
        for half in range(2):
            def step(i, run):
                g = half * HALF_BLK + i
                feats = jnp.concatenate([bt[r, rows_of(g)] for r in rows], axis=0)
                for n, r in enumerate(rows):
                    pre[g, r, :] = run[n * 8 : n * 8 + 8]
                both = dot(jnp.concatenate(split2(feats), axis=0), xd[rows_of(g), :])
                both = both[: feats.shape[0]] + both[feats.shape[0] :]
                fresh = both[:, :W] + both[:, W:]
                return lanes[pl.ds(g, 1), :] * run + fresh

            run = lax.fori_loop(0, HALF_BLK, step, jnp.zeros((8 * len(tiles), W), F32))
            for n, (t, fo, so) in enumerate(tiles):
                place = ((second[t] + so) % 4) * 4 + (first[t] + fo) % 4
                msg[t, place, half * 8 : half * 8 + 8, :] = run[n * 8 : n * 8 + 8]

    def group(so, kind):
        sec = y + (x - y) * kind
        return pl.ds(pl.multiple_of(((sec + so) % 4) * 4, 4), 4)

    def swap(so):
        g = group(so, 1 - core)
        return to_other(msg.at[1 - core, g], sib.at[g], so)

    def ship(so):
        swap(so).wait_recv()
        sec = y + (x - y) * core
        lead = ((sec + so) % 4) * 4
        for i in range(4):
            p = lead + i
            own_l, own_u = msg[core, p, 0:8, :], msg[core, p, 8:16, :]
            sib_l, sib_u = sib[p, 0:8, :], sib[p, 8:16, :]
            comb[p, 0:8, :] = jnp.where(
                core == 1, mine[0:1, :] * sib_l + own_l, theirs[0:1, :] * own_l + sib_l
            )
            comb[p, 8:16, :] = jnp.where(
                core == 0, mine[1:2, :] * sib_u + own_u, theirs[1:2, :] * own_u + sib_u
            )

            @pl.when(p != z)
            def _():
                pltpu.make_async_remote_copy(
                    comb.at[p], recv.at[z], asem.at[0], asem.at[1],
                    device_id={"seq": p * 2 + core}, device_id_type=MESH,
                ).start()

            @pl.when(p == z)
            def _():
                recv[p] = comb[p]

    def spread(src, dst, k):
        for off in (8, 9, 7, 10, 6, 11, 5, 12, 4, 13, 3, 14, 2, 15, 1):
            to = (z + off) % NZ
            pltpu.make_async_remote_copy(
                src(to), dst.at[z], asem.at[k], asem.at[k + 1],
                device_id={"seq": to * 2 + core}, device_id_type=MESH,
            ).start()

    def arrived(buf, k):
        part = buf.at[pl.ds(0, NZ - 1)]
        pltpu.make_async_copy(part, part, asem.at[k]).wait()

    def keys(g, _):
        khi[:, rows_of(g)], klo[:, rows_of(g)] = split2(bt[:, rows_of(g)])
        return 0

    last = len(PIECES) - 1

    def rest(p):
        for q in (1, 2, 3):
            cst[p].ev3(q)

    own[1].wait()
    hear(0)
    tell(1)
    bst.ev1()
    lax.fori_loop(0, 3, decay, 0)
    bst.ev3(0)
    bst.ev2()
    own[2].wait()
    cst[0].ev0()
    hear(1)
    tell(2)
    states((0,))
    swap(0).start()
    to_other(mine, theirs, 4).wait_recv()
    pair[...] = mine[...] * theirs[...]
    dk[z] = pair[...]
    lax.fori_loop(3, 6, decay, 0)
    for q in (1, 2, 3):
        bst.ev3(q)
    cst[0].ev1()
    cst[1].ev0()
    hear(2)
    spread(lambda to: pair, dk, 4)
    states((1, 3))
    swap(1).start()
    swap(3).start()
    ship(0)
    bst.ev4()
    states((2,))
    swap(2).start()
    ship(1)
    ship(3)
    ship(2)
    cst[0].ev3(0)
    cst[0].ev2()
    cst[1].ev1()
    lax.fori_loop(6, 11, decay, 0)
    rest(0)
    if last > 1:
        cst[2].ev0()
    lax.fori_loop(11, NBLK, decay, 0)
    lax.fori_loop(0, 4, keys, 0)
    def put(p, kind, tile):
        shard = p + ((p % 4) * 4 + p // 4 - p) * kind
        r = pl.ds(pl.multiple_of(shard * 16 + kind * 8, 8), 8)
        inc[0, r, :] = tile[0:8]
        inc[1, r, :] = tile[8:16]

    def enter_chip(p, _):
        low, high = ret[p, 0:8, :], ret[p, 8:16, :]
        own_l = mine[0:1, :] * low + msg[core, p, 0:8, :]
        own_u = mine[1:2, :] * high + msg[core, p, 8:16, :]
        sib_l = theirs[0:1, :] * low + sib[p, 0:8, :]
        sib_u = theirs[1:2, :] * high + sib[p, 8:16, :]
        give[p, 0:8, :] = jnp.where(core == 0, own_l, low)
        give[p, 8:16, :] = jnp.where(core == 0, high, own_u)
        put(p, core, jnp.concatenate(
            [jnp.where(core == 0, low, sib_l), jnp.where(core == 0, sib_u, high)], axis=0))
        return 0

    def enter_other(p, _):
        put(p, 1 - core, got[p])
        return 0

    arrived(dk, 5)
    arrived(recv, 1)
    run = jnp.zeros((8, W), F32)
    for j in range(NZ):
        incs[j, 0:8, :] = run
        run = dk[j, 0:1, :] * run + recv[j, 0:8, :]
    for j in reversed(range(NZ)):
        incs[j, 8:16, :] = run
        run = dk[j, 1:2, :] * run + recv[j, 8:16, :]
    spread(lambda to: incs.at[to], ret, 2)
    ret[z] = incs[z]

    cst[1].ev3(0)
    cst[1].ev2()
    lax.fori_loop(4, NBLK, keys, 0)
    cst[0].ev4()

    def inside(g):
        turned = ct[:, rows_of(g)].T
        qhi, qlo = split2(turned)
        chi[rows_of(g), :], clo[rows_of(g), :] = qhi, qlo
        scores = dot3(qhi, qlo, khi[:, rows_of(g)], klo[:, rows_of(g)])
        sums = []
        for h in range(2):
            weights = jnp.concatenate(split2(scores * dec[g, h]), axis=1)
            vals = xs[h, rows_of(g), :]
            sums.append(dot(weights, jnp.concatenate([vals, vals], axis=0)))
        out[rows_of(g), :] = jnp.where(first_head, sums[0], sums[1]) + pltpu.roll(
            jnp.where(first_head, sums[1], sums[0]), 64, 1
        )

    def carried(g):
        half = g // HALF_BLK
        enter = lanes[pl.ds(16 + g, 1), :] * inc[half] + pre[g]
        ehi, elo = split2(enter)
        part = dot(chi[rows_of(g), :], jnp.concatenate([ehi, elo], axis=1))
        part = part[:, :W] + (part[:, W:] + dot(clo[rows_of(g), :], ehi))
        out[rows_of(g), :] = out[rows_of(g), :] + ecum[rows_of(g), :] * part

    def only_inside(g, _):
        inside(g)
        return 0

    def only_carried(g, _):
        carried(g)
        return 0

    for p in range(last):
        groups = [lambda p=p: rest(p + 1)]
        if p + 3 <= last:
            groups[0] = lambda p=p: (rest(p + 1), cst[p + 3].ev0())
        if p + 2 <= last:
            groups += [cst[p + 2].ev1, lambda p=p: (cst[p + 2].ev3(0), cst[p + 2].ev2())]
        g = starts[p] // L
        for events in groups:
            inside(g)
            g += 1
            events()
        lax.fori_loop(g, starts[p + 1] // L, only_inside, 0, unroll=2)
        if p + 1 < last:
            cst[p + 1].ev4()
    cst[last].ev4()
    lax.fori_loop(starts[last] // L, NBLK, only_inside, 0, unroll=2)
    arrived(ret, 3)
    lax.fori_loop(0, NZ, enter_chip, 0, unroll=4)
    to_other(give, got, 5).start()
    to_other(give, got, 5).wait_recv()
    lax.fori_loop(0, NZ, enter_other, 0, unroll=4)
    halves = []
    for i in range(2):
        lax.fori_loop(i * HALF_BLK, (i + 1) * HALF_BLK, only_carried, 0, unroll=4)
        part = pl.ds(i * TOK // 2, TOK // 2)
        halves.append(pltpu.make_async_copy(out.at[part], o_ref.at[part], osem.at[i]))
        halves[-1].start()

    for i, buf in enumerate((bt, ct)):
        sent = buf.at[pl.ds(0, 240)]
        pltpu.make_async_copy(sent, sent, ssem.at[i]).wait()
    for i, buf in ((0, comb), (2, incs), (4, dk)):
        arrived(buf, i)
    for so in range(4):
        swap(so).wait_send()
    to_other(mine, theirs, 4).wait_send()
    to_other(give, got, 5).wait_send()
    for copy in halves:
        copy.wait()


def on_device(inputs, b_proj, c_proj, log_decay):
    vm = pltpu.VMEM
    return pl.pallas_call(
        kernel,
        out_shape=jax.ShapeDtypeStruct((TOK, W), F32),
        in_specs=[pl.BlockSpec(memory_space=pl.ANY)] * 3 + [pl.BlockSpec(memory_space=vm)],
        out_specs=pl.BlockSpec(memory_space=pl.ANY),
        scratch_shapes=[
            vm((N, TOK), F32), vm((N, TOK), F32),
            vm((TOK, W), F32),
            vm((2, TOK, W), BF16),
            vm((TOK, 2 * W), BF16),
            vm((TOK, N), BF16), vm((TOK, N), BF16),
            vm((N, TOK), BF16), vm((N, TOK), BF16),
            vm((NBLK, 2, L, L), F32),
            vm((TOK, W), F32),
            vm((NBLK, N, W), F32),
            vm((TOK, W), F32),
            vm((W, L), F32),
            vm((3, L, W), BF16),
            vm((32, W), F32),
            vm((2, NZ, 16, W), F32), vm((NZ, 16, W), F32),
            vm((NZ, 16, W), F32), vm((NZ, 16, W), F32),
            vm((NZ, 16, W), F32), vm((NZ, 16, W), F32),
            vm((NZ, 16, W), F32), vm((NZ, 16, W), F32),
            vm((2, N, W), F32),
            vm((8, W), F32), vm((8, W), F32), vm((8, W), F32),
            vm((NZ, 8, W), F32),
            pltpu.SemaphoreType.DMA((2,)),
            pltpu.SemaphoreType.DMA((32 * (1 + len(PIECES)),)),
            pltpu.SemaphoreType.DMA((3,)),
            pltpu.SemaphoreType.DMA((2,)),
            pltpu.SemaphoreType.DMA((6,)),
            pltpu.SemaphoreType.DMA((2, 6)),
            pltpu.SemaphoreType.REGULAR((3,)),
        ],
        compiler_params=pltpu.CompilerParams(
            collective_id=0, has_side_effects=True, vmem_limit_bytes=54 * 2**20
        ),
        cost_estimate=pl.CostEstimate(flops=5 * 10**9, bytes_accessed=2**23, transcendentals=3 * 10**6),
    )(inputs, b_proj.T, c_proj.T, log_decay.T)


def solution(mesh):
    return jax.shard_map(
        on_device,
        mesh=mesh,
        in_specs=(P("seq", "head"), P("seq", "head"), P("seq", "head"), P("seq", "head")),
        out_specs=P("seq", "head"),
        check_vma=False,
    )
```
